512 devices in a mesh: wide: 64 (over y_lo, z, core), narrow: 8 (over y_hi, x).
Axes of the slice: x: 4, y: 8 (y_hi: 2, y_lo: 4; y = y_hi * 4 + y_lo), z: 8, core: 2. Of those that a mesh axis runs over, the one named last changes fastest.
Arguments:
- query_values: bfloat16 [896, 1024], P('wide'), may hold values from -64 to 64
- query_scales: float32 [896, 32], P('wide'), may hold values from 0.2 to 4.5
- reference_rows: bfloat16 [49152, 1024], P(('wide', 'narrow')), may hold values from -12 to 12
Outputs:
- row_match: bfloat16 [896, 1024], P('wide')
- column_match: bfloat16 [49152, 1024], P(('wide', 'narrow'))
The draws below stay inside these ranges and needn't reach their ends.
All inputs are finite; a program needn't handle non-finite values.
Results may differ from the reference program's by a relative error of at most 0.01195.
Values may be sent and summed in bfloat16 or wider, within the bound.
No kernel may reach another device: no remote copies, remote signals or barrier semaphores. Data moves between devices by JAX's collectives and lax.ppermute only.
A program may use at most 64 MiB of HBM per device.

```python
import math
import jax
import jax.numpy as jnp
from jax import lax

D = 1024
GROUP = 32
REF_DEV = 96
NQ = 896
NR = 49152


def build_all(key):
    base = jax.random.fold_in(key, 41)
    keys = jax.random.split(base, 6)
    ref_scale = jnp.exp(jax.random.uniform(keys[0], (NR,), jnp.float32, jnp.log(0.4), jnp.log(4.0)))
    refs = jax.random.normal(keys[2], (NR, D), jnp.float32) * ref_scale[:, None]
    row_part = jnp.exp(jax.random.uniform(keys[3], (NQ,), jnp.float32, jnp.log(0.3), jnp.log(3.0)))
    group_part = jnp.exp(jax.random.uniform(keys[4], (NQ, D // GROUP), jnp.float32, jnp.log(0.7), jnp.log(1.4)))
    scales = row_part[:, None] * group_part
    expanded = jnp.repeat(scales, GROUP, axis=1)
    queries = jnp.clip(jax.random.normal(keys[5], (NQ, D), jnp.float32), -6.0, 6.0) * expanded
    refs = jnp.clip(refs, -12.0, 12.0)
    values = jnp.clip(queries / expanded, -64.0, 64.0)
    return (values, scales, refs)


def draw_query_values(key, part):
    return build_all(key)[0].astype(jnp.bfloat16)


def draw_query_scales(key, part):
    return build_all(key)[1].astype(jnp.float32)


def draw_reference_rows(key, part):
    return build_all(key)[2].astype(jnp.bfloat16)


def setup_inputs(seed: int = 0) -> dict:
    key_of = jax.random.split(jax.random.key(seed), 4)
    return {
        "query_values": draw_query_values(jax.random.fold_in(key_of[3], 71), 0),
        "query_scales": draw_query_scales(jax.random.fold_in(key_of[3], 71), 0),
        "reference_rows": draw_reference_rows(jax.random.fold_in(key_of[3], 71), 0),
    }


def dequantize(values, scales):
    rows, width = values.shape
    groups = scales.shape[1]
    spread = values.astype(jnp.float32).reshape(rows, groups, width // groups) * scales[:, :, None]
    return spread.reshape(rows, width).astype(jnp.bfloat16)

def reference(query_values, query_scales, reference_rows):
    queries = dequantize(query_values, query_scales)
    factor = 1.0 / math.sqrt(D)
    blocks = reference_rows.reshape(NR // REF_DEV, REF_DEV, D)

    def scan_block(carry, block):
        row_max, row_sum, row_acc = carry
        scores = lax.dot_general(queries, block, (((1,), (1,)), ((), ())), preferred_element_type=jnp.float32) * factor
        fresh = jnp.maximum(row_max, lax.optimization_barrier(jnp.max(scores, axis=1)))
        shrink = jnp.exp(row_max - fresh)
        weights = jnp.exp(scores - fresh[:, None])
        row_sum = row_sum * shrink + lax.optimization_barrier(jnp.sum(weights, axis=1))
        row_acc = row_acc * shrink[:, None] + jnp.dot(weights.astype(jnp.bfloat16), block, preferred_element_type=jnp.float32)
        col_max = lax.optimization_barrier(jnp.max(scores, axis=0))
        col_exp = jnp.exp(scores - col_max[None, :])
        col_sum = lax.optimization_barrier(jnp.sum(col_exp, axis=0))
        col_acc = lax.dot_general(col_exp.astype(jnp.bfloat16), queries, (((0,), (0,)), ((), ())), preferred_element_type=jnp.float32)
        return ((fresh, row_sum, row_acc), (col_acc / col_sum[:, None]).astype(jnp.bfloat16))
    start = (jnp.full((NQ,), -jnp.inf, jnp.float32), jnp.zeros((NQ,), jnp.float32), jnp.zeros((NQ, D), jnp.float32))
    (row_max, row_sum, row_acc), columns = lax.scan(scan_block, start, blocks)
    row_match = (row_acc / row_sum[:, None]).astype(jnp.bfloat16)
    return (row_match, columns.reshape(NR, D))
```

```python
import functools

import jax
import jax.numpy as jnp
from jax import lax
from jax.experimental import pallas as pl
from jax.experimental.pallas import tpu as pltpu
from jax.sharding import Mesh, PartitionSpec as P

FINE = (("yl", 4), ("z", 8), ("c", 2), ("yh", 2), ("xh", 2), ("xl", 2))
WIDE = ("yl", "z", "c")
NARROW = ("yh", "xh", "xl")
CHIPS = ("yl", "z")

D = 1024
STATS = 128
MSG = D + STATS
SLOT = 8
BIG = 1e30
BF = jnp.bfloat16
F32 = jnp.float32


def lanes(rows):
    return lax.broadcasted_iota(jnp.int32, (rows, STATS), 1)


def split(x):
    hi = x.astype(BF).astype(F32)
    rest = x - hi
    mid = rest.astype(BF).astype(F32)
    return hi, mid, (rest - mid).astype(BF).astype(F32)


def stats_of(top, total):
    rows = top.shape[0]
    lane = lanes(rows)
    out = jnp.zeros((rows, STATS), F32)
    for k, part in enumerate(split(top) + split(total)):
        out = jnp.where(lane == k, part, out)
    return out


def read_stats(stats):
    lane = lanes(stats.shape[0])
    top = jnp.sum(jnp.where(lane < 3, stats, 0.0), axis=1, keepdims=True)
    total = jnp.sum(jnp.where((lane >= 3) & (lane < 6), stats, 0.0), axis=1, keepdims=True)
    return top, total


def softmax_parts(scores):
    top = jnp.max(scores, axis=1, keepdims=True)
    weights = jnp.exp(scores - top)
    return top, jnp.sum(weights, axis=1, keepdims=True), weights.astype(BF)


def match_kernel(q_ref, mine_ref, theirs_ref, bias_ref, row_ref, keep_ref, send_ref, refs):
    half = mine_ref.shape[0]
    refs[:half] = mine_ref[...]
    refs[half:] = theirs_ref[...]
    q = q_ref[...]
    nt = (((1,), (1,)), ((), ()))
    scores = lax.dot_general(q, refs[...], nt, preferred_element_type=F32) * (1.0 / 32.0)
    top, total, weights = softmax_parts(scores)
    row_ref[:, :D] = jnp.dot(weights, refs[...], preferred_element_type=F32).astype(BF)
    row_ref[:, D:] = stats_of(top, total).astype(BF)
    columns = lax.dot_general(refs[...], q, nt, preferred_element_type=F32) * (1.0 / 32.0)
    top, total, weights = softmax_parts(columns + bias_ref[...])
    stats = stats_of(top, total)
    keep_ref[:, :D] = jnp.dot(weights[:half], q, preferred_element_type=F32)
    keep_ref[:, D:] = stats[:half]
    send_ref[:, :D] = jnp.dot(weights[half:], q, preferred_element_type=F32).astype(BF)
    send_ref[:, D:] = stats[half:].astype(BF)


def joined_pair(a, b):
    top_a, total_a = read_stats(a[:, D:])
    top_b, total_b = read_stats(b[:, D:])
    top = jnp.maximum(top_a, top_b)
    left, right = jnp.exp(top_a - top), jnp.exp(top_b - top)
    return top, total_a * left + total_b * right, a[:, :D] * left + b[:, :D] * right


def joined_slots(msgs, count):
    top, total = read_stats(msgs[:, D:])
    top = top.reshape(count, SLOT, 1)
    best = jnp.max(top, axis=0, keepdims=True)
    scale = jnp.exp(top - best)
    acc = jnp.sum(msgs[:, :D].reshape(count, SLOT, D) * scale, axis=0)
    return best[0], jnp.sum(total.reshape(count, SLOT, 1) * scale, axis=0), acc


def middle_kernel(count, copies, rows_ref, keep_ref, came_ref, out_ref, kept_ref, send_ref):
    top, total, acc = joined_slots(rows_ref[...].astype(F32), count)
    message = jnp.concatenate([acc, stats_of(top, total)], axis=1)
    message = jnp.broadcast_to(message[None], (copies, SLOT, MSG)).reshape(copies * SLOT, MSG)
    out_ref[...] = message.astype(BF)
    own = kept_ref.shape[0]
    top, total, acc = joined_pair(keep_ref[...], came_ref[...].astype(F32))
    stats = stats_of(top, total)
    kept_ref[:, :D] = acc[:own]
    kept_ref[:, D:] = stats[:own]
    send_ref[:, :D] = acc[own:].astype(BF)
    send_ref[:, D:] = stats[own:].astype(BF)


def last_kernel(count, rows_ref, kept_ref, came_ref, row_ref, column_ref):
    msgs = rows_ref[...].astype(F32).reshape(count // 2, 2, SLOT, MSG)
    parts = []
    for k in range(2):
        _, total, acc = joined_slots(msgs[:, k].reshape(count // 2 * SLOT, MSG), count // 2)
        parts.append(acc / total)
    rows = row_ref.shape[0]
    row_ref[...] = jnp.concatenate(parts, axis=0)[:rows].astype(BF)
    _, total, acc = joined_pair(kept_ref[...], came_ref[...].astype(F32))
    column_ref[...] = (acc / total).astype(BF)


def call(kernel, shapes, *args, scratch=()):
    vmem = pl.BlockSpec(memory_space=pltpu.VMEM)
    return pl.pallas_call(
        kernel,
        out_shape=[jax.ShapeDtypeStruct(s, t) for s, t in shapes],
        in_specs=[vmem] * len(args),
        out_specs=[vmem] * len(shapes),
        scratch_shapes=list(scratch),
        compiler_params=pltpu.CompilerParams(vmem_limit_bytes=32 * 1024 * 1024),
    )(*args)


def swapped(x, axis):
    return lax.ppermute(x, axis, [(0, 1), (1, 0)])


def dequantize(values, scales):
    rows, width = values.shape
    groups = scales.shape[1]
    spread = values.astype(F32).reshape(rows, groups, width // groups) * scales[:, :, None]
    return spread.reshape(rows, width).astype(BF)


def per_device(query_values, query_scales, reference_rows):
    rows = query_values.shape[0]
    own = reference_rows.shape[0]
    chips = lax.axis_size(CHIPS)
    narrow = lax.axis_size(NARROW)
    parity = lax.axis_index("xl")

    mine = jnp.concatenate([reference_rows, swapped(reference_rows, "c")], axis=0)
    theirs = swapped(mine, "xl")

    queries = dequantize(query_values, query_scales)
    upper = jnp.pad(queries[SLOT:], ((0, 2 * SLOT - rows), (0, 0)))
    slot = jnp.where(parity == 0, queries[:SLOT], upper)
    gathered = lax.all_to_all(jnp.broadcast_to(slot[None], (chips, SLOT, D)), CHIPS, 0, 0)
    gathered = gathered.reshape(chips * SLOT, D)
    place = lax.broadcasted_iota(jnp.int32, (1, chips * SLOT), 1) % SLOT + parity * SLOT
    bias = jnp.where(place < rows, 0.0, -BIG).astype(F32)

    row_msg, keep, send = call(
        match_kernel,
        [((chips * SLOT, MSG), BF), ((2 * own, MSG), F32), ((2 * own, MSG), BF)],
        gathered,
        mine,
        theirs,
        bias,
        scratch=[pltpu.VMEM((4 * own, D), BF)],
    )
    came = swapped(send, "xl")
    row_parts = lax.all_to_all(row_msg.reshape(chips, SLOT, MSG), CHIPS, 0, 0)
    row_msg, kept, send = call(
        functools.partial(middle_kernel, chips, narrow),
        [((narrow * SLOT, MSG), BF), ((own, MSG), F32), ((own, MSG), BF)],
        row_parts.reshape(chips * SLOT, MSG),
        keep,
        came,
    )
    came = swapped(send, "c")
    row_parts = lax.all_to_all(row_msg.reshape(narrow, SLOT, MSG), NARROW, 0, 0)
    return tuple(
        call(
            functools.partial(last_kernel, narrow),
            [((rows, D), BF), ((own, D), BF)],
            row_parts.reshape(narrow * SLOT, MSG),
            kept,
            came,
        )
    )


def solution(mesh):
    fine = Mesh(mesh.devices.reshape([n for _, n in FINE]), tuple(a for a, _ in FINE))
    return jax.shard_map(
        per_device,
        mesh=fine,
        in_specs=(P(WIDE, None), P(WIDE, None), P(WIDE + NARROW, None)),
        out_specs=(P(WIDE, None), P(WIDE + NARROW, None)),
        check_vma=False,
    )
```

```python
import functools

import jax
import jax.numpy as jnp
from jax import lax
from jax.experimental import pallas as pl
from jax.experimental.pallas import tpu as pltpu
from jax.sharding import Mesh, PartitionSpec as P

FINE = (("yl", 4), ("z", 8), ("c", 2), ("yh", 2), ("xh", 2), ("xl", 2))
WIDE = ("yl", "z", "c")
NARROW = ("yh", "xh", "xl")
CHIPS = ("yl", "z")

D = 1024
STATS = 128
MSG = D + STATS
SLOT = 8
TAKEN = SLOT - 1
BIG = 1e30
BF = jnp.bfloat16
F32 = jnp.float32


def lanes(rows):
    return lax.broadcasted_iota(jnp.int32, (rows, STATS), 1)


def split(x):
    hi = x.astype(BF).astype(F32)
    rest = x - hi
    mid = rest.astype(BF).astype(F32)
    return hi, mid, (rest - mid).astype(BF).astype(F32)


def stats_of(top, total):
    rows = top.shape[0]
    lane = lanes(rows)
    out = jnp.zeros((rows, STATS), F32)
    for k, part in enumerate(split(top) + split(total)):
        out = jnp.where(lane == k, part, out)
    return out


def read_stats(stats):
    lane = lanes(stats.shape[0])
    top = jnp.sum(jnp.where(lane < 3, stats, 0.0), axis=1, keepdims=True)
    total = jnp.sum(jnp.where((lane >= 3) & (lane < 6), stats, 0.0), axis=1, keepdims=True)
    return top, total


def softmax_parts(scores):
    top = jnp.max(scores, axis=1, keepdims=True)
    weights = jnp.exp(scores - top)
    return top, jnp.sum(weights, axis=1, keepdims=True), weights.astype(BF)


def spread_kernel(values_hbm, scales_hbm, first_ref, out_hbm, values_ref, scales_ref, slots_ref, arrived, left):
    loads = [
        pltpu.make_async_copy(values_hbm, values_ref, arrived.at[0]),
        pltpu.make_async_copy(scales_hbm, scales_ref, arrived.at[1]),
    ]
    for load in loads:
        load.start()
    groups = scales_ref.shape[1]
    column = lax.broadcasted_iota(jnp.int32, (groups, D), 1)
    start = lax.broadcasted_iota(jnp.int32, (groups, D), 0) * (D // groups)
    ones = jnp.where((column >= start) & (column < start + D // groups), 1.0, 0.0).astype(BF)
    for load in loads:
        load.wait()
    scales = sum(
        jnp.dot(part.astype(BF), ones, preferred_element_type=F32) for part in split(scales_ref[...])
    )
    queries = values_ref[...].astype(F32) * scales
    slot = jnp.where(first_ref[...] > 0.0, queries[:TAKEN], queries[TAKEN : 2 * TAKEN])
    slot = jnp.concatenate([slot, jnp.zeros((1, D), F32)] * 2, axis=0)
    slots_ref[...] = slot.astype(BF)
    height = slots_ref.shape[0]
    stores = [
        pltpu.make_async_copy(slots_ref, out_hbm.at[pl.ds(k * height, height)], left.at[k])
        for k in range(out_hbm.shape[0] // height)
    ]
    for store in stores:
        store.start()
    for store in stores:
        store.wait()


def slot_row(shape):
    return lax.broadcasted_iota(jnp.int32, shape, len(shape) - 2)


def with_stats(k, part, stats):
    if k >= TAKEN:
        return part
    return jnp.where(slot_row(part.shape) == TAKEN, stats[:, k : k + 1], part)


def read_slots(msgs):
    stats = jnp.zeros((*msgs.shape[:2], STATS), F32)
    for k in range(TAKEN):
        stats = jnp.where(slot_row(stats.shape) == k, msgs[:, TAKEN:, k * STATS : (k + 1) * STATS], stats)
    return stats


NT = (((1,), (1,)), ((), ()))


def row_kernel(q_ref, refs_ref, row_hbm, row_ref, left):
    scores = lax.dot_general(q_ref[...], refs_ref[...], NT, preferred_element_type=F32) * (1.0 / 32.0)
    top, total, weights = softmax_parts(scores)
    stats = stats_of(top, total).reshape(-1, SLOT, STATS)
    width = D // left.shape[0]
    stores = []
    for at in range(0, D, width):
        acc = jnp.dot(weights, refs_ref[:, at : at + width], preferred_element_type=F32)
        for k in range(at // STATS, (at + width) // STATS):
            part = acc[:, k * STATS - at : (k + 1) * STATS - at].reshape(-1, SLOT, STATS)
            part = with_stats(k, part, stats).reshape(-1, STATS)
            row_ref[:, k * STATS : (k + 1) * STATS] = part.astype(BF)
        columns = pl.ds(at, width)
        store = pltpu.make_async_copy(row_ref.at[:, columns], row_hbm.at[:, columns], left.at[len(stores)])
        store.start()
        stores.append(store)
    for store in stores:
        store.wait()


def column_kernel(q_ref, refs_ref, keep_ref, send_ref):
    half = keep_ref.shape[0]
    q = q_ref[...]
    place = lax.broadcasted_iota(jnp.int32, (1, q.shape[0]), 1) % SLOT
    bias = jnp.where(place < TAKEN, 0.0, -BIG)
    scores = lax.dot_general(refs_ref[...], q, NT, preferred_element_type=F32) * (1.0 / 32.0)
    top, total, weights = softmax_parts(scores + bias)
    acc = jnp.dot(weights, q, preferred_element_type=F32)
    stats = stats_of(top, total)
    keep_ref[:, :D] = acc[:half]
    keep_ref[:, D:] = stats[:half]
    send_ref[:, :D] = acc[half:].astype(BF)
    send_ref[:, D:] = stats[half:].astype(BF)


def joined_pair(a, b):
    top_a, total_a = read_stats(a[:, D:])
    top_b, total_b = read_stats(b[:, D:])
    top = jnp.maximum(top_a, top_b)
    left, right = jnp.exp(top_a - top), jnp.exp(top_b - top)
    return top, total_a * left + total_b * right, a[:, :D] * left + b[:, :D] * right


def joined_slots(msgs):
    count = msgs.shape[0]
    top, total = read_stats(read_slots(msgs).reshape(count * SLOT, STATS))
    top = top.reshape(count, SLOT, 1)
    best = jnp.max(top, axis=0, keepdims=True)
    scale = jnp.exp(top - best)
    return best[0], jnp.sum(total.reshape(count, SLOT, 1) * scale, axis=0), jnp.sum(msgs * scale, axis=0)


def middle_kernel(count, copies, rows_ref, out_ref):
    top, total, acc = joined_slots(rows_ref[...].astype(F32).reshape(count, SLOT, D))
    stats = stats_of(top, total)[None]
    for k in range(D // STATS):
        columns = pl.ds(k * STATS, STATS)
        part = with_stats(k, acc[None, :, k * STATS : (k + 1) * STATS], stats)
        part = jnp.broadcast_to(part, (copies, SLOT, STATS)).reshape(copies * SLOT, STATS)
        out_ref[:, columns] = part.astype(BF)


def column_join_kernel(keep_ref, came_ref, kept_ref, send_ref):
    own = kept_ref.shape[0]
    top, total, acc = joined_pair(keep_ref[...], came_ref[...].astype(F32))
    stats = stats_of(top, total)
    kept_ref[:, :D] = acc[:own]
    kept_ref[:, D:] = stats[:own]
    send_ref[:, :D] = acc[own:].astype(BF)
    send_ref[:, D:] = stats[own:].astype(BF)


def last_kernel(count, rows_ref, kept_ref, came_ref, row_ref, column_ref):
    msgs = rows_ref[...].astype(F32).reshape(count // 2, 2, SLOT, D)
    parts = []
    for k in range(2):
        _, total, acc = joined_slots(msgs[:, k])
        parts.append(acc[:TAKEN] / total[:TAKEN])
    row_ref[...] = jnp.concatenate(parts, axis=0).astype(BF)
    _, total, acc = joined_pair(kept_ref[...], came_ref[...].astype(F32))
    column_ref[...] = (acc / total).astype(BF)


def call(kernel, shapes, *args, scratch=(), flops=0, far=(), far_out=(), limit=32):
    place = {True: pl.BlockSpec(memory_space=pltpu.HBM), False: pl.BlockSpec(memory_space=pltpu.VMEM)}
    sizes = [a.size * a.dtype.itemsize for a in args]
    return pl.pallas_call(
        kernel,
        out_shape=[jax.ShapeDtypeStruct(s, t) for s, t in shapes],
        in_specs=[place[k in far] for k in range(len(args))],
        out_specs=[place[k in far_out] for k in range(len(shapes))],
        scratch_shapes=list(scratch),
        cost_estimate=pl.CostEstimate(flops=flops, bytes_accessed=2 * sum(sizes), transcendentals=0),
        compiler_params=pltpu.CompilerParams(vmem_limit_bytes=limit * 1024 * 1024),
    )(*args)


def swapped(x, axis):
    return lax.ppermute(x, axis, [(0, 1), (1, 0)])


def per_device(query_values, query_scales, reference_rows):
    rows = query_values.shape[0]
    own = reference_rows.shape[0]
    chips = lax.axis_size(CHIPS)
    narrow = lax.axis_size(NARROW)
    parity = lax.axis_index("xl")

    near = swapped(reference_rows, "xl")
    core = swapped(jnp.concatenate([reference_rows, near], axis=0), "c")

    first = jnp.full((1, 1), 1.0 - parity.astype(F32), F32)
    (slots,) = call(
        spread_kernel,
        [((chips * SLOT, D), BF)],
        query_values,
        query_scales,
        first,
        scratch=[
            pltpu.VMEM(query_values.shape, BF),
            pltpu.VMEM(query_scales.shape, F32),
            pltpu.VMEM((2 * SLOT, D), BF),
            pltpu.SemaphoreType.DMA((2,)),
            pltpu.SemaphoreType.DMA((chips // 2,)),
        ],
        far=(0, 1),
        far_out=(0,),
        limit=60,
    )
    gathered = lax.all_to_all(slots.reshape(chips, SLOT, D), CHIPS, 0, 0).reshape(chips * SLOT, D)
    flops = 2 * 2 * chips * SLOT * 4 * own * D
    refs = jnp.concatenate([reference_rows, near, core], axis=0)
    (row_msg,) = call(
        row_kernel,
        [((chips * SLOT, D), BF)],
        gathered,
        refs,
        scratch=[pltpu.VMEM((chips * SLOT, D), BF), pltpu.SemaphoreType.DMA((4,))],
        flops=flops,
        far_out=(0,),
    )
    row_parts = lax.all_to_all(row_msg.reshape(chips, SLOT, D), CHIPS, 0, 0)
    keep, send = call(
        column_kernel,
        [((2 * own, MSG), F32), ((2 * own, MSG), BF)],
        gathered,
        refs,
        flops=flops,
    )
    kept, send = call(
        column_join_kernel, [((own, MSG), F32), ((own, MSG), BF)], keep, swapped(send, "c")
    )
    row_parts, kept, came = lax.optimization_barrier((row_parts, kept, swapped(send, "xl")))

    (row_msg,) = call(
        functools.partial(middle_kernel, chips, narrow),
        [((narrow * SLOT, D), BF)],
        row_parts.reshape(chips * SLOT, D),
    )
    row_parts = lax.all_to_all(row_msg.reshape(narrow, SLOT, D), NARROW, 0, 0)
    return tuple(
        call(
            functools.partial(last_kernel, narrow),
            [((rows, D), BF), ((own, D), BF)],
            row_parts.reshape(narrow * SLOT, D),
            kept,
            came,
        )
    )


def solution(mesh):
    fine = Mesh(mesh.devices.reshape([n for _, n in FINE]), tuple(a for a, _ in FINE))
    return jax.shard_map(
        per_device,
        mesh=fine,
        in_specs=(P(WIDE, None), P(WIDE, None), P(WIDE + NARROW, None)),
        out_specs=(P(WIDE, None), P(WIDE + NARROW, None)),
        check_vma=False,
    )
```

```python
import functools

import jax
import jax.numpy as jnp
from jax import lax
from jax.experimental import pallas as pl
from jax.experimental.pallas import tpu as pltpu
from jax.sharding import Mesh, PartitionSpec as P

FINE = (("yl", 4), ("z", 8), ("c", 2), ("yh", 2), ("xh", 2), ("xl", 2))
WIDE = ("yl", "z", "c")
NARROW = ("yh", "xh", "xl")
CHIPS = ("yl", "z")

D = 1024
STATS = 128
MSG = D + STATS
SLOT = 8
TAKEN = SLOT - 1
SENT = TAKEN * 128
BIG = 1e30
BF = jnp.bfloat16
F32 = jnp.float32


def lanes(rows):
    return lax.broadcasted_iota(jnp.int32, (rows, STATS), 1)


def split(x):
    hi = x.astype(BF).astype(F32)
    rest = x - hi
    mid = rest.astype(BF).astype(F32)
    return hi, mid, (rest - mid).astype(BF).astype(F32)


def stats_of(top, total):
    rows = top.shape[0]
    lane = lanes(rows)
    out = jnp.zeros((rows, STATS), F32)
    for k, part in enumerate(split(top) + split(total)):
        out = jnp.where(lane == k, part, out)
    return out


def read_stats(stats):
    lane = lanes(stats.shape[0])
    top = jnp.sum(jnp.where(lane < 3, stats, 0.0), axis=1, keepdims=True)
    total = jnp.sum(jnp.where((lane >= 3) & (lane < 6), stats, 0.0), axis=1, keepdims=True)
    return top, total


def softmax_parts(scores):
    top = jnp.max(scores, axis=1, keepdims=True)
    weights = jnp.exp(scores - top)
    return top, jnp.sum(weights, axis=1, keepdims=True), weights.astype(BF)


def spread_kernel(values_hbm, scales_hbm, first_ref, out_hbm, values_ref, scales_ref, slots_ref, arrived, left):
    loads = [
        pltpu.make_async_copy(values_hbm, values_ref, arrived.at[0]),
        pltpu.make_async_copy(scales_hbm, scales_ref, arrived.at[1]),
    ]
    for load in loads:
        load.start()
    groups = scales_ref.shape[1]
    column = lax.broadcasted_iota(jnp.int32, (groups, D), 1)
    start = lax.broadcasted_iota(jnp.int32, (groups, D), 0) * (D // groups)
    ones = jnp.where((column >= start) & (column < start + D // groups), 1.0, 0.0).astype(BF)
    for load in loads:
        load.wait()
    scales = sum(
        jnp.dot(part.astype(BF), ones, preferred_element_type=F32) for part in split(scales_ref[...])
    )
    queries = values_ref[...].astype(F32) * scales
    slot = jnp.where(first_ref[...] > 0.0, queries[:TAKEN], queries[TAKEN : 2 * TAKEN])
    slot = jnp.concatenate([slot, jnp.zeros((1, D), F32)], axis=0)[None]
    height = slots_ref.shape[0]
    for k in range(TAKEN):
        part = with_stats(k, slot[:, :, k * STATS : (k + 1) * STATS], slot[:, :, SENT:])
        part = jnp.broadcast_to(part, (height // SLOT, SLOT, STATS)).reshape(height, STATS)
        slots_ref[:, k * STATS : (k + 1) * STATS] = part.astype(BF)
    stores = [
        pltpu.make_async_copy(slots_ref, out_hbm.at[pl.ds(k * height, height)], left.at[k])
        for k in range(out_hbm.shape[0] // height)
    ]
    for store in stores:
        store.start()
    for store in stores:
        store.wait()


def slot_row(shape):
    return lax.broadcasted_iota(jnp.int32, shape, len(shape) - 2)


def with_stats(k, part, stats):
    if k >= TAKEN:
        return part
    return jnp.where(slot_row(part.shape) == TAKEN, stats[:, k : k + 1], part)


def read_slots(msgs):
    stats = jnp.zeros((*msgs.shape[:2], STATS), F32)
    for k in range(TAKEN):
        stats = jnp.where(slot_row(stats.shape) == k, msgs[:, TAKEN:, k * STATS : (k + 1) * STATS], stats)
    return stats


NT = (((1,), (1,)), ((), ()))


def row_kernel(sent_ref, refs_ref, row_hbm, q_ref, row_ref, left):
    sent = sent_ref[...]
    q_ref[:, :SENT] = sent
    q_ref[:, SENT:] = read_slots(sent.astype(F32).reshape(-1, SLOT, SENT)).reshape(-1, STATS).astype(BF)
    scores = lax.dot_general(q_ref[...], refs_ref[...], NT, preferred_element_type=F32) * (1.0 / 32.0)
    top, total, weights = softmax_parts(scores)
    stats = stats_of(top, total).reshape(-1, SLOT, STATS)
    width = D // left.shape[0]
    stores = []
    for at in range(0, D, width):
        acc = jnp.dot(weights, refs_ref[:, at : at + width], preferred_element_type=F32)
        for k in range(at // STATS, (at + width) // STATS):
            part = acc[:, k * STATS - at : (k + 1) * STATS - at].reshape(-1, SLOT, STATS)
            part = with_stats(k, part, stats).reshape(-1, STATS)
            row_ref[:, k * STATS : (k + 1) * STATS] = part.astype(BF)
        columns = pl.ds(at, width)
        store = pltpu.make_async_copy(row_ref.at[:, columns], row_hbm.at[:, columns], left.at[len(stores)])
        store.start()
        stores.append(store)
    for store in stores:
        store.wait()


def column_kernel(q_ref, refs_ref, keep_ref, send_ref):
    half = keep_ref.shape[0]
    q = q_ref[...]
    place = lax.broadcasted_iota(jnp.int32, (1, q.shape[0]), 1) % SLOT
    bias = jnp.where(place < TAKEN, 0.0, -BIG)
    scores = lax.dot_general(refs_ref[...], q, NT, preferred_element_type=F32) * (1.0 / 32.0)
    top, total, weights = softmax_parts(scores + bias)
    acc = jnp.dot(weights, q, preferred_element_type=F32)
    stats = stats_of(top, total)
    keep_ref[:, :D] = acc[:half]
    keep_ref[:, D:] = stats[:half]
    send_ref[:, :D] = acc[half:].astype(BF)
    send_ref[:, D:] = stats[half:].astype(BF)


def joined_pair(a, b):
    top_a, total_a = read_stats(a[:, D:])
    top_b, total_b = read_stats(b[:, D:])
    top = jnp.maximum(top_a, top_b)
    left, right = jnp.exp(top_a - top), jnp.exp(top_b - top)
    return top, total_a * left + total_b * right, a[:, :D] * left + b[:, :D] * right


def joined_slots(msgs):
    count = msgs.shape[0]
    top, total = read_stats(read_slots(msgs).reshape(count * SLOT, STATS))
    top = top.reshape(count, SLOT, 1)
    best = jnp.max(top, axis=0, keepdims=True)
    scale = jnp.exp(top - best)
    return best[0], jnp.sum(total.reshape(count, SLOT, 1) * scale, axis=0), jnp.sum(msgs * scale, axis=0)


def middle_kernel(count, copies, rows_ref, out_ref):
    top, total, acc = joined_slots(rows_ref[...].astype(F32).reshape(count, SLOT, D))
    stats = stats_of(top, total)[None]
    for k in range(D // STATS):
        columns = pl.ds(k * STATS, STATS)
        part = with_stats(k, acc[None, :, k * STATS : (k + 1) * STATS], stats)
        part = jnp.broadcast_to(part, (copies, SLOT, STATS)).reshape(copies * SLOT, STATS)
        out_ref[:, columns] = part.astype(BF)


def column_join_kernel(keep_ref, came_ref, kept_ref, send_ref):
    own = kept_ref.shape[0]
    top, total, acc = joined_pair(keep_ref[...], came_ref[...].astype(F32))
    stats = stats_of(top, total)
    kept_ref[:, :D] = acc[:own]
    kept_ref[:, D:] = stats[:own]
    send_ref[:, :D] = acc[own:].astype(BF)
    send_ref[:, D:] = stats[own:].astype(BF)


def last_kernel(count, rows_ref, kept_ref, came_ref, row_ref, column_ref):
    msgs = rows_ref[...].astype(F32).reshape(count // 2, 2, SLOT, D)
    parts = []
    for k in range(2):
        _, total, acc = joined_slots(msgs[:, k])
        parts.append(acc[:TAKEN] / total[:TAKEN])
    row_ref[...] = jnp.concatenate(parts, axis=0).astype(BF)
    _, total, acc = joined_pair(kept_ref[...], came_ref[...].astype(F32))
    column_ref[...] = (acc / total).astype(BF)


def call(kernel, shapes, *args, scratch=(), flops=0, far=(), far_out=(), limit=32):
    place = {True: pl.BlockSpec(memory_space=pltpu.HBM), False: pl.BlockSpec(memory_space=pltpu.VMEM)}
    sizes = [a.size * a.dtype.itemsize for a in args]
    return pl.pallas_call(
        kernel,
        out_shape=[jax.ShapeDtypeStruct(s, t) for s, t in shapes],
        in_specs=[place[k in far] for k in range(len(args))],
        out_specs=[place[k in far_out] for k in range(len(shapes))],
        scratch_shapes=list(scratch),
        cost_estimate=pl.CostEstimate(flops=flops, bytes_accessed=2 * sum(sizes), transcendentals=0),
        compiler_params=pltpu.CompilerParams(vmem_limit_bytes=limit * 1024 * 1024),
    )(*args)


def swapped(x, axis):
    return lax.ppermute(x, axis, [(0, 1), (1, 0)])


def per_device(query_values, query_scales, reference_rows):
    rows = query_values.shape[0]
    own = reference_rows.shape[0]
    chips = lax.axis_size(CHIPS)
    narrow = lax.axis_size(NARROW)
    parity = lax.axis_index("xl")

    near = swapped(reference_rows, "xl")
    core = swapped(reference_rows, "c")
    core_near = swapped(near, "c")

    first = jnp.full((1, 1), 1.0 - parity.astype(F32), F32)
    (slots,) = call(
        spread_kernel,
        [((chips * SLOT, SENT), BF)],
        query_values,
        query_scales,
        first,
        scratch=[
            pltpu.VMEM(query_values.shape, BF),
            pltpu.VMEM(query_scales.shape, F32),
            pltpu.VMEM((8 * SLOT, SENT), BF),
            pltpu.SemaphoreType.DMA((2,)),
            pltpu.SemaphoreType.DMA((chips // 8,)),
        ],
        far=(0, 1),
        far_out=(0,),
        limit=60,
    )
    gathered = lax.all_to_all(slots.reshape(chips, SLOT, SENT), CHIPS, 0, 0).reshape(chips * SLOT, SENT)
    flops = 2 * 2 * chips * SLOT * 4 * own * D
    refs = jnp.concatenate([reference_rows, near, core, core_near], axis=0)
    row_msg, queries = call(
        row_kernel,
        [((chips * SLOT, D), BF), ((chips * SLOT, D), BF)],
        gathered,
        refs,
        scratch=[pltpu.VMEM((chips * SLOT, D), BF), pltpu.SemaphoreType.DMA((4,))],
        flops=flops,
        far_out=(0,),
    )
    row_parts = lax.all_to_all(row_msg.reshape(chips, SLOT, D), CHIPS, 0, 0)
    keep, send = call(
        column_kernel,
        [((2 * own, MSG), F32), ((2 * own, MSG), BF)],
        queries,
        refs,
        flops=flops,
    )
    kept, send = call(
        column_join_kernel, [((own, MSG), F32), ((own, MSG), BF)], keep, swapped(send, "c")
    )
    row_parts, kept = lax.optimization_barrier((row_parts, kept))
    came = swapped(send, "xl")

    (row_msg,) = call(
        functools.partial(middle_kernel, chips, narrow),
        [((narrow * SLOT, D), BF)],
        row_parts.reshape(chips * SLOT, D),
    )
    always = lax.optimization_barrier(jnp.bool_(True))
    row_parts = lax.cond(
        always, lambda x: lax.all_to_all(x, NARROW, 0, 0), lambda x: x, row_msg.reshape(narrow, SLOT, D)
    )
    return tuple(
        call(
            functools.partial(last_kernel, narrow),
            [((rows, D), BF), ((own, D), BF)],
            row_parts.reshape(narrow * SLOT, D),
            kept,
            came,
        )
    )


def solution(mesh):
    fine = Mesh(mesh.devices.reshape([n for _, n in FINE]), tuple(a for a, _ in FINE))
    return jax.shard_map(
        per_device,
        mesh=fine,
        in_specs=(P(WIDE, None), P(WIDE, None), P(WIDE + NARROW, None)),
        out_specs=(P(WIDE, None), P(WIDE + NARROW, None)),
        check_vma=False,
    )
```

```python
import functools

import jax
import jax.numpy as jnp
from jax import lax
from jax.experimental import pallas as pl
from jax.experimental.pallas import tpu as pltpu
from jax.sharding import PartitionSpec as P

CHIPS = [[(y * 8 + z) * 2 + core for y in range(4) for z in reversed(range(8))] for core in range(2)]
ACROSS = [[6, 7, 4, 5, 2, 3, 0, 1]]

D = 1024
STATS = 128
MSG = D + STATS
SLOT = 8
TAKEN = SLOT - 1
SENT = TAKEN * 128
BIG = 1e30
BF = jnp.bfloat16
F32 = jnp.float32


def lanes(rows):
    return lax.broadcasted_iota(jnp.int32, (rows, STATS), 1)


def split(x):
    hi = x.astype(BF).astype(F32)
    rest = x - hi
    mid = rest.astype(BF).astype(F32)
    return hi, mid, (rest - mid).astype(BF).astype(F32)


def stats_of(top, total):
    rows = top.shape[0]
    lane = lanes(rows)
    out = jnp.zeros((rows, STATS), F32)
    for k, part in enumerate(split(top) + split(total)):
        out = jnp.where(lane == k, part, out)
    return out


def read_stats(stats):
    lane = lanes(stats.shape[0])
    top = jnp.sum(jnp.where(lane < 3, stats, 0.0), axis=1, keepdims=True)
    total = jnp.sum(jnp.where((lane >= 3) & (lane < 6), stats, 0.0), axis=1, keepdims=True)
    return top, total


def softmax_parts(scores):
    top = jnp.max(scores, axis=1, keepdims=True)
    weights = jnp.exp(scores - top)
    return top, jnp.sum(weights, axis=1, keepdims=True), weights.astype(BF)


def spread_kernel(values_hbm, scales_hbm, first_ref, out_hbm, values_ref, scales_ref, slots_ref, arrived, left):
    loads = [
        pltpu.make_async_copy(values_hbm, values_ref, arrived.at[0]),
        pltpu.make_async_copy(scales_hbm, scales_ref, arrived.at[1]),
    ]
    for load in loads:
        load.start()
    groups = scales_ref.shape[1]
    column = lax.broadcasted_iota(jnp.int32, (groups, D), 1)
    start = lax.broadcasted_iota(jnp.int32, (groups, D), 0) * (D // groups)
    ones = jnp.where((column >= start) & (column < start + D // groups), 1.0, 0.0).astype(BF)
    for load in loads:
        load.wait()
    scales = sum(
        jnp.dot(part.astype(BF), ones, preferred_element_type=F32) for part in split(scales_ref[...])
    )
    queries = values_ref[...].astype(F32) * scales
    slot = jnp.where(first_ref[...] > 0.0, queries[:TAKEN], queries[TAKEN : 2 * TAKEN])
    slot = jnp.concatenate([slot, jnp.zeros((1, D), F32)], axis=0)[None]
    height = slots_ref.shape[0]
    for k in range(TAKEN):
        part = with_stats(k, slot[:, :, k * STATS : (k + 1) * STATS], slot[:, :, SENT:])
        part = jnp.broadcast_to(part, (height // SLOT, SLOT, STATS)).reshape(height, STATS)
        slots_ref[:, k * STATS : (k + 1) * STATS] = part.astype(BF)
    stores = [
        pltpu.make_async_copy(slots_ref, out_hbm.at[pl.ds(k * height, height)], left.at[k])
        for k in range(out_hbm.shape[0] // height)
    ]
    for store in stores:
        store.start()
    for store in stores:
        store.wait()


def slot_row(shape):
    return lax.broadcasted_iota(jnp.int32, shape, len(shape) - 2)


def with_stats(k, part, stats):
    if k >= TAKEN:
        return part
    return jnp.where(slot_row(part.shape) == TAKEN, stats[:, k : k + 1], part)


def read_slots(msgs):
    stats = jnp.zeros((*msgs.shape[:2], STATS), F32)
    for k in range(TAKEN):
        stats = jnp.where(slot_row(stats.shape) == k, msgs[:, TAKEN:, k * STATS : (k + 1) * STATS], stats)
    return stats


NT = (((1,), (1,)), ((), ()))


def row_kernel(sent_ref, refs_ref, row_hbm, q_ref, row_ref, left):
    sent = sent_ref[...]
    q_ref[:, :SENT] = sent
    q_ref[:, SENT:] = read_slots(sent.astype(F32).reshape(-1, SLOT, SENT)).reshape(-1, STATS).astype(BF)
    scores = lax.dot_general(q_ref[...], refs_ref[...], NT, preferred_element_type=F32) * (1.0 / 32.0)
    top, total, weights = softmax_parts(scores)
    stats = stats_of(top, total).reshape(-1, SLOT, STATS)
    width = D // left.shape[0]
    stores = []
    for at in range(0, D, width):
        acc = jnp.dot(weights, refs_ref[:, at : at + width], preferred_element_type=F32)
        for k in range(at // STATS, (at + width) // STATS):
            part = acc[:, k * STATS - at : (k + 1) * STATS - at].reshape(-1, SLOT, STATS)
            part = with_stats(k, part, stats).reshape(-1, STATS)
            row_ref[:, k * STATS : (k + 1) * STATS] = part.astype(BF)
        columns = pl.ds(at, width)
        store = pltpu.make_async_copy(row_ref.at[:, columns], row_hbm.at[:, columns], left.at[len(stores)])
        store.start()
        stores.append(store)
    for store in stores:
        store.wait()


def column_kernel(q_ref, refs_ref, keep_ref, send_ref):
    half = keep_ref.shape[0]
    q = q_ref[...]
    place = lax.broadcasted_iota(jnp.int32, (1, q.shape[0]), 1) % SLOT
    bias = jnp.where(place < TAKEN, 0.0, -BIG)
    scores = lax.dot_general(refs_ref[...], q, NT, preferred_element_type=F32) * (1.0 / 32.0)
    top, total, weights = softmax_parts(scores + bias)
    acc = jnp.dot(weights, q, preferred_element_type=F32)
    stats = stats_of(top, total)
    keep_ref[:, :D] = acc[:half]
    keep_ref[:, D:] = stats[:half]
    send_ref[:, :D] = acc[half:].astype(BF)
    send_ref[:, D:] = stats[half:].astype(BF)


def joined_pair(a, b):
    top_a, total_a = read_stats(a[:, D:])
    top_b, total_b = read_stats(b[:, D:])
    top = jnp.maximum(top_a, top_b)
    left, right = jnp.exp(top_a - top), jnp.exp(top_b - top)
    return top, total_a * left + total_b * right, a[:, :D] * left + b[:, :D] * right


def joined_slots(msgs):
    count = msgs.shape[0]
    top, total = read_stats(read_slots(msgs).reshape(count * SLOT, STATS))
    top = top.reshape(count, SLOT, 1)
    best = jnp.max(top, axis=0, keepdims=True)
    scale = jnp.exp(top - best)
    return best[0], jnp.sum(total.reshape(count, SLOT, 1) * scale, axis=0), jnp.sum(msgs * scale, axis=0)


def middle_kernel(count, copies, rows_ref, out_ref):
    top, total, acc = joined_slots(rows_ref[...].astype(F32).reshape(count, SLOT, D))
    stats = stats_of(top, total)[None]
    for k in range(D // STATS):
        columns = pl.ds(k * STATS, STATS)
        part = with_stats(k, acc[None, :, k * STATS : (k + 1) * STATS], stats)
        part = jnp.broadcast_to(part, (copies, SLOT, STATS)).reshape(copies * SLOT, STATS)
        out_ref[:, columns] = part.astype(BF)


def column_join_kernel(keep_ref, came_ref, kept_ref, send_ref):
    own = kept_ref.shape[0]
    top, total, acc = joined_pair(keep_ref[...], came_ref[...].astype(F32))
    stats = stats_of(top, total)
    kept_ref[:, :D] = acc[:own]
    kept_ref[:, D:] = stats[:own]
    send_ref[:, :D] = acc[own:].astype(BF)
    send_ref[:, D:] = stats[own:].astype(BF)


def last_kernel(count, rows_ref, kept_ref, came_ref, row_ref, column_ref):
    msgs = rows_ref[...].astype(F32).reshape(count // 2, 2, SLOT, D)
    parts = []
    for k in range(2):
        _, total, acc = joined_slots(msgs[:, k])
        parts.append(acc[:TAKEN] / total[:TAKEN])
    row_ref[...] = jnp.concatenate(parts, axis=0).astype(BF)
    _, total, acc = joined_pair(kept_ref[...], came_ref[...].astype(F32))
    column_ref[...] = (acc / total).astype(BF)


def call(kernel, shapes, *args, scratch=(), flops=0, far=(), far_out=(), limit=32):
    place = {True: pl.BlockSpec(memory_space=pltpu.HBM), False: pl.BlockSpec(memory_space=pltpu.VMEM)}
    sizes = [a.size * a.dtype.itemsize for a in args]
    return pl.pallas_call(
        kernel,
        out_shape=[jax.ShapeDtypeStruct(s, t) for s, t in shapes],
        in_specs=[place[k in far] for k in range(len(args))],
        out_specs=[place[k in far_out] for k in range(len(shapes))],
        scratch_shapes=list(scratch),
        cost_estimate=pl.CostEstimate(flops=flops, bytes_accessed=2 * sum(sizes), transcendentals=0),
        compiler_params=pltpu.CompilerParams(vmem_limit_bytes=limit * 1024 * 1024),
    )(*args)


def swapped(x, axis):
    return lax.ppermute(x, axis, [(k, k ^ 1) for k in range(lax.axis_size(axis))])


def exchanged(x, axis, groups):
    return lax.all_to_all(x, axis, 0, 0, axis_index_groups=groups)


def per_device(query_values, query_scales, reference_rows):
    rows = query_values.shape[0]
    own = reference_rows.shape[0]
    chips = lax.axis_size("wide") // 2
    narrow = lax.axis_size("narrow")
    parity = lax.axis_index("narrow") % 2

    near = swapped(reference_rows, "narrow")
    core = swapped(reference_rows, "wide")
    core_near = swapped(near, "wide")

    first = jnp.full((1, 1), 1.0 - parity.astype(F32), F32)
    (slots,) = call(
        spread_kernel,
        [((chips * SLOT, SENT), BF)],
        query_values,
        query_scales,
        first,
        scratch=[
            pltpu.VMEM(query_values.shape, BF),
            pltpu.VMEM(query_scales.shape, F32),
            pltpu.VMEM((8 * SLOT, SENT), BF),
            pltpu.SemaphoreType.DMA((2,)),
            pltpu.SemaphoreType.DMA((chips // 8,)),
        ],
        far=(0, 1),
        far_out=(0,),
        limit=60,
    )
    gathered = exchanged(slots.reshape(chips, SLOT, SENT), "wide", CHIPS).reshape(chips * SLOT, SENT)
    flops = 2 * 2 * chips * SLOT * 4 * own * D
    refs = jnp.concatenate([reference_rows, near, core, core_near], axis=0)
    row_msg, queries = call(
        row_kernel,
        [((chips * SLOT, D), BF), ((chips * SLOT, D), BF)],
        gathered,
        refs,
        scratch=[pltpu.VMEM((chips * SLOT, D), BF), pltpu.SemaphoreType.DMA((4,))],
        flops=flops,
        far_out=(0,),
    )
    row_parts = exchanged(row_msg.reshape(chips, SLOT, D), "wide", CHIPS)
    keep, send = call(
        column_kernel,
        [((2 * own, MSG), F32), ((2 * own, MSG), BF)],
        queries,
        refs,
        flops=flops,
    )
    kept, send = call(
        column_join_kernel, [((own, MSG), F32), ((own, MSG), BF)], keep, swapped(send, "wide")
    )
    row_parts, kept = lax.optimization_barrier((row_parts, kept))
    came = swapped(send, "narrow")

    (row_msg,) = call(
        functools.partial(middle_kernel, chips, narrow),
        [((narrow * SLOT, D), BF)],
        row_parts.reshape(chips * SLOT, D),
    )
    always = lax.optimization_barrier(jnp.bool_(True))
    row_parts = lax.cond(
        always, lambda x: exchanged(x, "narrow", ACROSS), lambda x: x, row_msg.reshape(narrow, SLOT, D)
    )
    return tuple(
        call(
            functools.partial(last_kernel, narrow),
            [((rows, D), BF), ((own, D), BF)],
            row_parts.reshape(narrow * SLOT, D),
            kept,
            came,
        )
    )


def solution(mesh):
    return jax.shard_map(
        per_device,
        mesh=mesh,
        in_specs=(P("wide", None), P("wide", None), P(("wide", "narrow"), None)),
        out_specs=(P("wide", None), P(("wide", "narrow"), None)),
        check_vma=False,
    )
```

```python
import functools

import jax
import jax.numpy as jnp
from jax import lax
from jax.experimental import pallas as pl
from jax.experimental.pallas import tpu as pltpu
from jax.sharding import PartitionSpec as P

CHIPS = [[(y * 8 + z) * 2 + core for y in (1, 0, 2, 3) for z in reversed(range(8))] for core in range(2)]
ACROSS = [[6, 7, 4, 5, 2, 3, 0, 1]]

D = 1024
STATS = 128
MSG = D + STATS
SLOT = 8
TAKEN = SLOT - 1
SENT = TAKEN * 128
BIG = 1e30
BF = jnp.bfloat16
F32 = jnp.float32


def lanes(rows):
    return lax.broadcasted_iota(jnp.int32, (rows, STATS), 1)


def split(x):
    hi = x.astype(BF).astype(F32)
    rest = x - hi
    mid = rest.astype(BF).astype(F32)
    return hi, mid, (rest - mid).astype(BF).astype(F32)


def stats_of(top, total):
    rows = top.shape[0]
    lane = lanes(rows)
    out = jnp.zeros((rows, STATS), F32)
    for k, part in enumerate(split(top) + split(total)):
        out = jnp.where(lane == k, part, out)
    return out


def read_stats(stats):
    lane = lanes(stats.shape[0])
    top = jnp.sum(jnp.where(lane < 3, stats, 0.0), axis=1, keepdims=True)
    total = jnp.sum(jnp.where((lane >= 3) & (lane < 6), stats, 0.0), axis=1, keepdims=True)
    return top, total


def softmax_parts(scores):
    top = jnp.max(scores, axis=1, keepdims=True)
    weights = jnp.exp(scores - top)
    return top, jnp.sum(weights, axis=1, keepdims=True), weights.astype(BF)


def spread_kernel(values_hbm, scales_hbm, first_ref, out_hbm, values_ref, scales_ref, slots_ref, arrived, left):
    loads = [
        pltpu.make_async_copy(values_hbm, values_ref, arrived.at[0]),
        pltpu.make_async_copy(scales_hbm, scales_ref, arrived.at[1]),
    ]
    for load in loads:
        load.start()
    groups = scales_ref.shape[1]
    column = lax.broadcasted_iota(jnp.int32, (groups, D), 1)
    start = lax.broadcasted_iota(jnp.int32, (groups, D), 0) * (D // groups)
    ones = jnp.where((column >= start) & (column < start + D // groups), 1.0, 0.0).astype(BF)
    for load in loads:
        load.wait()
    scales = sum(
        jnp.dot(part.astype(BF), ones, preferred_element_type=F32) for part in split(scales_ref[...])
    )
    queries = values_ref[...].astype(F32) * scales
    slot = jnp.where(first_ref[...] > 0.0, queries[:TAKEN], queries[TAKEN : 2 * TAKEN])
    slot = jnp.concatenate([slot, jnp.zeros((1, D), F32)], axis=0)[None]
    height = slots_ref.shape[0]
    for k in range(TAKEN):
        part = with_stats(k, slot[:, :, k * STATS : (k + 1) * STATS], slot[:, :, SENT:])
        part = jnp.broadcast_to(part, (height // SLOT, SLOT, STATS)).reshape(height, STATS)
        slots_ref[:, k * STATS : (k + 1) * STATS] = part.astype(BF)
    stores = [
        pltpu.make_async_copy(slots_ref, out_hbm.at[pl.ds(k * height, height)], left.at[k])
        for k in range(out_hbm.shape[0] // height)
    ]
    for store in stores:
        store.start()
    for store in stores:
        store.wait()


def slot_row(shape):
    return lax.broadcasted_iota(jnp.int32, shape, len(shape) - 2)


def with_stats(k, part, stats):
    if k >= TAKEN:
        return part
    return jnp.where(slot_row(part.shape) == TAKEN, stats[:, k : k + 1], part)


def read_slots(msgs):
    stats = jnp.zeros((*msgs.shape[:2], STATS), F32)
    for k in range(TAKEN):
        stats = jnp.where(slot_row(stats.shape) == k, msgs[:, TAKEN:, k * STATS : (k + 1) * STATS], stats)
    return stats


NT = (((1,), (1,)), ((), ()))


def row_kernel(sent_ref, refs_ref, row_hbm, q_ref, row_ref, left):
    sent = sent_ref[...]
    q_ref[:, :SENT] = sent
    q_ref[:, SENT:] = read_slots(sent.astype(F32).reshape(-1, SLOT, SENT)).reshape(-1, STATS).astype(BF)
    scores = lax.dot_general(q_ref[...], refs_ref[...], NT, preferred_element_type=F32) * (1.0 / 32.0)
    top, total, weights = softmax_parts(scores)
    stats = stats_of(top, total).reshape(-1, SLOT, STATS)
    width = D // left.shape[0]
    stores = []
    for at in range(0, D, width):
        acc = jnp.dot(weights, refs_ref[:, at : at + width], preferred_element_type=F32)
        for k in range(at // STATS, (at + width) // STATS):
            part = acc[:, k * STATS - at : (k + 1) * STATS - at].reshape(-1, SLOT, STATS)
            part = with_stats(k, part, stats).reshape(-1, STATS)
            row_ref[:, k * STATS : (k + 1) * STATS] = part.astype(BF)
        columns = pl.ds(at, width)
        store = pltpu.make_async_copy(row_ref.at[:, columns], row_hbm.at[:, columns], left.at[len(stores)])
        store.start()
        stores.append(store)
    for store in stores:
        store.wait()


def column_kernel(q_ref, refs_ref, keep_ref, send_ref):
    half = keep_ref.shape[0]
    q = q_ref[...]
    place = lax.broadcasted_iota(jnp.int32, (1, q.shape[0]), 1) % SLOT
    bias = jnp.where(place < TAKEN, 0.0, -BIG)
    scores = lax.dot_general(refs_ref[...], q, NT, preferred_element_type=F32) * (1.0 / 32.0)
    top, total, weights = softmax_parts(scores + bias)
    acc = jnp.dot(weights, q, preferred_element_type=F32)
    stats = stats_of(top, total)
    keep_ref[:, :D] = acc[:half]
    keep_ref[:, D:] = stats[:half]
    send_ref[:, :D] = acc[half:].astype(BF)
    send_ref[:, D:] = stats[half:].astype(BF)


def joined_pair(a, b):
    top_a, total_a = read_stats(a[:, D:])
    top_b, total_b = read_stats(b[:, D:])
    top = jnp.maximum(top_a, top_b)
    left, right = jnp.exp(top_a - top), jnp.exp(top_b - top)
    return top, total_a * left + total_b * right, a[:, :D] * left + b[:, :D] * right


def joined_slots(msgs):
    count = msgs.shape[0]
    top, total = read_stats(read_slots(msgs).reshape(count * SLOT, STATS))
    top = top.reshape(count, SLOT, 1)
    best = jnp.max(top, axis=0, keepdims=True)
    scale = jnp.exp(top - best)
    return best[0], jnp.sum(total.reshape(count, SLOT, 1) * scale, axis=0), jnp.sum(msgs * scale, axis=0)


def middle_kernel(count, copies, rows_ref, out_ref):
    top, total, acc = joined_slots(rows_ref[...].astype(F32).reshape(count, SLOT, D))
    stats = stats_of(top, total)[None]
    for k in range(D // STATS):
        columns = pl.ds(k * STATS, STATS)
        part = with_stats(k, acc[None, :, k * STATS : (k + 1) * STATS], stats)
        part = jnp.broadcast_to(part, (copies, SLOT, STATS)).reshape(copies * SLOT, STATS)
        out_ref[:, columns] = part.astype(BF)


def column_join_kernel(keep_ref, came_ref, kept_ref, send_ref):
    own = kept_ref.shape[0]
    top, total, acc = joined_pair(keep_ref[...], came_ref[...].astype(F32))
    stats = stats_of(top, total)
    kept_ref[:, :D] = acc[:own]
    kept_ref[:, D:] = stats[:own]
    send_ref[:, :D] = acc[own:].astype(BF)
    send_ref[:, D:] = stats[own:].astype(BF)


def last_kernel(count, rows_ref, kept_ref, came_ref, row_ref, column_ref):
    msgs = rows_ref[...].astype(F32).reshape(count // 2, 2, SLOT, D)
    parts = []
    for k in range(2):
        _, total, acc = joined_slots(msgs[:, k])
        parts.append(acc[:TAKEN] / total[:TAKEN])
    row_ref[...] = jnp.concatenate(parts, axis=0).astype(BF)
    _, total, acc = joined_pair(kept_ref[...], came_ref[...].astype(F32))
    column_ref[...] = (acc / total).astype(BF)


def call(kernel, shapes, *args, scratch=(), flops=0, far=(), far_out=(), limit=32):
    place = {True: pl.BlockSpec(memory_space=pltpu.HBM), False: pl.BlockSpec(memory_space=pltpu.VMEM)}
    sizes = [a.size * a.dtype.itemsize for a in args]
    return pl.pallas_call(
        kernel,
        out_shape=[jax.ShapeDtypeStruct(s, t) for s, t in shapes],
        in_specs=[place[k in far] for k in range(len(args))],
        out_specs=[place[k in far_out] for k in range(len(shapes))],
        scratch_shapes=list(scratch),
        cost_estimate=pl.CostEstimate(flops=flops, bytes_accessed=2 * sum(sizes), transcendentals=0),
        compiler_params=pltpu.CompilerParams(vmem_limit_bytes=limit * 1024 * 1024),
    )(*args)


def swapped(x, axis):
    return lax.ppermute(x, axis, [(k, k ^ 1) for k in range(lax.axis_size(axis))])


def exchanged(x, axis, groups):
    return lax.all_to_all(x, axis, 0, 0, axis_index_groups=groups)


def per_device(query_values, query_scales, reference_rows):
    rows = query_values.shape[0]
    own = reference_rows.shape[0]
    chips = lax.axis_size("wide") // 2
    narrow = lax.axis_size("narrow")
    parity = lax.axis_index("narrow") % 2

    near = swapped(reference_rows, "narrow")
    core = swapped(reference_rows, "wide")
    core_near = swapped(near, "wide")

    first = jnp.full((1, 1), 1.0 - parity.astype(F32), F32)
    (slots,) = call(
        spread_kernel,
        [((chips * SLOT, SENT), BF)],
        query_values,
        query_scales,
        first,
        scratch=[
            pltpu.VMEM(query_values.shape, BF),
            pltpu.VMEM(query_scales.shape, F32),
            pltpu.VMEM((8 * SLOT, SENT), BF),
            pltpu.SemaphoreType.DMA((2,)),
            pltpu.SemaphoreType.DMA((chips // 8,)),
        ],
        far=(0, 1),
        far_out=(0,),
        limit=60,
    )
    gathered = exchanged(slots.reshape(chips, SLOT, SENT), "wide", CHIPS).reshape(chips * SLOT, SENT)
    flops = 2 * 2 * chips * SLOT * 4 * own * D
    refs = jnp.concatenate([reference_rows, near, core, core_near], axis=0)
    row_msg, queries = call(
        row_kernel,
        [((chips * SLOT, D), BF), ((chips * SLOT, D), BF)],
        gathered,
        refs,
        scratch=[pltpu.VMEM((chips * SLOT, D), BF), pltpu.SemaphoreType.DMA((4,))],
        flops=flops,
        far_out=(0,),
    )
    row_parts = exchanged(row_msg.reshape(chips, SLOT, D), "wide", CHIPS)
    keep, send = call(
        column_kernel,
        [((2 * own, MSG), F32), ((2 * own, MSG), BF)],
        queries,
        refs,
        flops=flops,
    )
    kept, send = call(
        column_join_kernel, [((own, MSG), F32), ((own, MSG), BF)], keep, swapped(send, "wide")
    )
    row_parts, kept = lax.optimization_barrier((row_parts, kept))
    came = swapped(send, "narrow")

    (row_msg,) = call(
        functools.partial(middle_kernel, chips, narrow),
        [((narrow * SLOT, D), BF)],
        row_parts.reshape(chips * SLOT, D),
    )
    always = lax.optimization_barrier(jnp.bool_(True))
    row_parts = lax.cond(
        always, lambda x: exchanged(x, "narrow", ACROSS), lambda x: x, row_msg.reshape(narrow, SLOT, D)
    )
    return tuple(
        call(
            functools.partial(last_kernel, narrow),
            [((rows, D), BF), ((own, D), BF)],
            row_parts.reshape(narrow * SLOT, D),
            kept,
            came,
        )
    )


def solution(mesh):
    return jax.shard_map(
        per_device,
        mesh=mesh,
        in_specs=(P("wide", None), P("wide", None), P(("wide", "narrow"), None)),
        out_specs=(P("wide", None), P(("wide", "narrow"), None)),
        check_vma=False,
    )
```

```python
import functools

import jax
import jax.numpy as jnp
from jax import lax
from jax.experimental import pallas as pl
from jax.experimental.pallas import tpu as pltpu
from jax.sharding import PartitionSpec as P

CHIPS = [[(y * 8 + z) * 2 + core for y in (1, 0, 2, 3) for z in reversed(range(8))] for core in range(2)]
BACK = [[g[k ^ 4] for k in range(32)] for g in CHIPS]
ACROSS = [[6, 7, 4, 5, 2, 3, 0, 1]]

D = 1024
STATS = 128
MSG = D + STATS
SLOT = 8
TAKEN = SLOT - 1
SENT = TAKEN * 128
BIG = 1e30
BF = jnp.bfloat16
F32 = jnp.float32


def lanes(rows):
    return lax.broadcasted_iota(jnp.int32, (rows, STATS), 1)


def split(x):
    hi = x.astype(BF).astype(F32)
    rest = x - hi
    mid = rest.astype(BF).astype(F32)
    return hi, mid, (rest - mid).astype(BF).astype(F32)


def stats_of(top, total):
    rows = top.shape[0]
    lane = lanes(rows)
    out = jnp.zeros((rows, STATS), F32)
    for k, part in enumerate(split(top) + split(total)):
        out = jnp.where(lane == k, part, out)
    return out


def read_stats(stats):
    lane = lanes(stats.shape[0])
    top = jnp.sum(jnp.where(lane < 3, stats, 0.0), axis=1, keepdims=True)
    total = jnp.sum(jnp.where((lane >= 3) & (lane < 6), stats, 0.0), axis=1, keepdims=True)
    return top, total


def softmax_parts(scores):
    top = jnp.max(scores, axis=1, keepdims=True)
    weights = jnp.exp(scores - top)
    return top, jnp.sum(weights, axis=1, keepdims=True), weights.astype(BF)


def spread_kernel(values_hbm, scales_hbm, first_ref, out_hbm, values_ref, scales_ref, slots_ref, arrived, left):
    loads = [
        pltpu.make_async_copy(values_hbm, values_ref, arrived.at[0]),
        pltpu.make_async_copy(scales_hbm, scales_ref, arrived.at[1]),
    ]
    for load in loads:
        load.start()
    groups = scales_ref.shape[1]
    column = lax.broadcasted_iota(jnp.int32, (groups, D), 1)
    start = lax.broadcasted_iota(jnp.int32, (groups, D), 0) * (D // groups)
    ones = jnp.where((column >= start) & (column < start + D // groups), 1.0, 0.0).astype(BF)
    for load in loads:
        load.wait()
    scales = sum(
        jnp.dot(part.astype(BF), ones, preferred_element_type=F32) for part in split(scales_ref[...])
    )
    queries = values_ref[...].astype(F32) * scales
    slot = jnp.where(first_ref[...] > 0.0, queries[:TAKEN], queries[TAKEN : 2 * TAKEN])
    slot = jnp.concatenate([slot, jnp.zeros((1, D), F32)], axis=0)[None]
    height = slots_ref.shape[0]
    for k in range(TAKEN):
        part = with_stats(k, slot[:, :, k * STATS : (k + 1) * STATS], slot[:, :, SENT:])
        part = jnp.broadcast_to(part, (height // SLOT, SLOT, STATS)).reshape(height, STATS)
        slots_ref[:, k * STATS : (k + 1) * STATS] = part.astype(BF)
    stores = [
        pltpu.make_async_copy(slots_ref, out_hbm.at[pl.ds(k * height, height)], left.at[k])
        for k in range(out_hbm.shape[0] // height)
    ]
    for store in stores:
        store.start()
    for store in stores:
        store.wait()


def slot_row(shape):
    return lax.broadcasted_iota(jnp.int32, shape, len(shape) - 2)


def with_stats(k, part, stats):
    if k >= TAKEN:
        return part
    return jnp.where(slot_row(part.shape) == TAKEN, stats[:, k : k + 1], part)


def read_slots(msgs):
    stats = jnp.zeros((*msgs.shape[:2], STATS), F32)
    for k in range(TAKEN):
        stats = jnp.where(slot_row(stats.shape) == k, msgs[:, TAKEN:, k * STATS : (k + 1) * STATS], stats)
    return stats


NT = (((1,), (1,)), ((), ()))


def row_kernel(sent_ref, refs_ref, row_hbm, q_ref, row_ref, left):
    half = 4 * SLOT
    sent = jnp.concatenate(
        [sent_ref[(k ^ 1) * half : (k ^ 1) * half + half] for k in range(sent_ref.shape[0] // half)], axis=0
    )
    q_ref[:, :SENT] = sent
    q_ref[:, SENT:] = read_slots(sent.astype(F32).reshape(-1, SLOT, SENT)).reshape(-1, STATS).astype(BF)
    scores = lax.dot_general(q_ref[...], refs_ref[...], NT, preferred_element_type=F32) * (1.0 / 32.0)
    top, total, weights = softmax_parts(scores)
    stats = stats_of(top, total).reshape(-1, SLOT, STATS)
    width = D // left.shape[0]
    stores = []
    for at in range(0, D, width):
        acc = jnp.dot(weights, refs_ref[:, at : at + width], preferred_element_type=F32)
        for k in range(at // STATS, (at + width) // STATS):
            part = acc[:, k * STATS - at : (k + 1) * STATS - at].reshape(-1, SLOT, STATS)
            part = with_stats(k, part, stats).reshape(-1, STATS)
            row_ref[:, k * STATS : (k + 1) * STATS] = part.astype(BF)
        columns = pl.ds(at, width)
        store = pltpu.make_async_copy(row_ref.at[:, columns], row_hbm.at[:, columns], left.at[len(stores)])
        store.start()
        stores.append(store)
    for store in stores:
        store.wait()


def column_kernel(q_ref, refs_ref, keep_ref, send_ref):
    half = keep_ref.shape[0]
    q = q_ref[...]
    place = lax.broadcasted_iota(jnp.int32, (1, q.shape[0]), 1) % SLOT
    bias = jnp.where(place < TAKEN, 0.0, -BIG)
    scores = lax.dot_general(refs_ref[...], q, NT, preferred_element_type=F32) * (1.0 / 32.0)
    top, total, weights = softmax_parts(scores + bias)
    acc = jnp.dot(weights, q, preferred_element_type=F32)
    stats = stats_of(top, total)
    keep_ref[:, :D] = acc[:half]
    keep_ref[:, D:] = stats[:half]
    send_ref[:, :D] = acc[half:].astype(BF)
    send_ref[:, D:] = stats[half:].astype(BF)


def joined_pair(a, b):
    top_a, total_a = read_stats(a[:, D:])
    top_b, total_b = read_stats(b[:, D:])
    top = jnp.maximum(top_a, top_b)
    left, right = jnp.exp(top_a - top), jnp.exp(top_b - top)
    return top, total_a * left + total_b * right, a[:, :D] * left + b[:, :D] * right


def joined_slots(msgs):
    count = msgs.shape[0]
    top, total = read_stats(read_slots(msgs).reshape(count * SLOT, STATS))
    top = top.reshape(count, SLOT, 1)
    best = jnp.max(top, axis=0, keepdims=True)
    scale = jnp.exp(top - best)
    return best[0], jnp.sum(total.reshape(count, SLOT, 1) * scale, axis=0), jnp.sum(msgs * scale, axis=0)


def middle_kernel(count, copies, rows_ref, out_ref):
    top, total, acc = joined_slots(rows_ref[...].astype(F32).reshape(count, SLOT, D))
    stats = stats_of(top, total)[None]
    for k in range(D // STATS):
        columns = pl.ds(k * STATS, STATS)
        part = with_stats(k, acc[None, :, k * STATS : (k + 1) * STATS], stats)
        part = jnp.broadcast_to(part, (copies, SLOT, STATS)).reshape(copies * SLOT, STATS)
        out_ref[:, columns] = part.astype(BF)


def column_join_kernel(keep_ref, came_ref, kept_ref, send_ref):
    own = kept_ref.shape[0]
    top, total, acc = joined_pair(keep_ref[...], came_ref[...].astype(F32))
    stats = stats_of(top, total)
    kept_ref[:, :D] = acc[:own]
    kept_ref[:, D:] = stats[:own]
    send_ref[:, :D] = acc[own:].astype(BF)
    send_ref[:, D:] = stats[own:].astype(BF)


def last_kernel(count, rows_ref, kept_ref, came_ref, row_ref, column_ref):
    msgs = rows_ref[...].astype(F32).reshape(count // 2, 2, SLOT, D)
    parts = []
    for k in range(2):
        _, total, acc = joined_slots(msgs[:, k])
        parts.append(acc[:TAKEN] / total[:TAKEN])
    row_ref[...] = jnp.concatenate(parts, axis=0).astype(BF)
    _, total, acc = joined_pair(kept_ref[...], came_ref[...].astype(F32))
    column_ref[...] = (acc / total).astype(BF)


def call(kernel, shapes, *args, scratch=(), flops=0, far=(), far_out=(), limit=32):
    place = {True: pl.BlockSpec(memory_space=pltpu.HBM), False: pl.BlockSpec(memory_space=pltpu.VMEM)}
    sizes = [a.size * a.dtype.itemsize for a in args]
    return pl.pallas_call(
        kernel,
        out_shape=[jax.ShapeDtypeStruct(s, t) for s, t in shapes],
        in_specs=[place[k in far] for k in range(len(args))],
        out_specs=[place[k in far_out] for k in range(len(shapes))],
        scratch_shapes=list(scratch),
        cost_estimate=pl.CostEstimate(flops=flops, bytes_accessed=2 * sum(sizes), transcendentals=0),
        compiler_params=pltpu.CompilerParams(vmem_limit_bytes=limit * 1024 * 1024),
    )(*args)


def swapped(x, axis):
    return lax.ppermute(x, axis, [(k, k ^ 1) for k in range(lax.axis_size(axis))])


def exchanged(x, axis, groups):
    return lax.all_to_all(x, axis, 0, 0, axis_index_groups=groups)


def per_device(query_values, query_scales, reference_rows):
    rows = query_values.shape[0]
    own = reference_rows.shape[0]
    chips = lax.axis_size("wide") // 2
    narrow = lax.axis_size("narrow")
    parity = lax.axis_index("narrow") % 2

    near = swapped(reference_rows, "narrow")
    core = swapped(reference_rows, "wide")
    core_near = swapped(near, "wide")

    first = jnp.full((1, 1), 1.0 - parity.astype(F32), F32)
    (slots,) = call(
        spread_kernel,
        [((chips * SLOT, SENT), BF)],
        query_values,
        query_scales,
        first,
        scratch=[
            pltpu.VMEM(query_values.shape, BF),
            pltpu.VMEM(query_scales.shape, F32),
            pltpu.VMEM((8 * SLOT, SENT), BF),
            pltpu.SemaphoreType.DMA((2,)),
            pltpu.SemaphoreType.DMA((chips // 8,)),
        ],
        far=(0, 1),
        far_out=(0,),
        limit=60,
    )
    gathered = exchanged(slots.reshape(chips, SLOT, SENT), "wide", CHIPS).reshape(chips * SLOT, SENT)
    flops = 2 * 2 * chips * SLOT * 4 * own * D
    refs = jnp.concatenate([reference_rows, near, core, core_near], axis=0)
    row_msg, queries = call(
        row_kernel,
        [((chips * SLOT, D), BF), ((chips * SLOT, D), BF)],
        gathered,
        refs,
        scratch=[pltpu.VMEM((chips * SLOT, D), BF), pltpu.SemaphoreType.DMA((4,))],
        flops=flops,
        far_out=(0,),
    )
    row_parts = exchanged(row_msg.reshape(chips, SLOT, D), "wide", BACK)
    keep, send = call(
        column_kernel,
        [((2 * own, MSG), F32), ((2 * own, MSG), BF)],
        queries,
        refs,
        flops=flops,
    )
    kept, send = call(
        column_join_kernel, [((own, MSG), F32), ((own, MSG), BF)], keep, swapped(send, "wide")
    )
    row_parts, kept = lax.optimization_barrier((row_parts, kept))
    came = swapped(send, "narrow")

    (row_msg,) = call(
        functools.partial(middle_kernel, chips, narrow),
        [((narrow * SLOT, D), BF)],
        row_parts.reshape(chips * SLOT, D),
    )
    always = lax.optimization_barrier(jnp.bool_(True))
    row_parts = lax.cond(
        always, lambda x: exchanged(x, "narrow", ACROSS), lambda x: x, row_msg.reshape(narrow, SLOT, D)
    )
    return tuple(
        call(
            functools.partial(last_kernel, narrow),
            [((rows, D), BF), ((own, D), BF)],
            row_parts.reshape(narrow * SLOT, D),
            kept,
            came,
        )
    )


def solution(mesh):
    return jax.shard_map(
        per_device,
        mesh=mesh,
        in_specs=(P("wide", None), P("wide", None), P(("wide", "narrow"), None)),
        out_specs=(P("wide", None), P(("wide", "narrow"), None)),
        check_vma=False,
    )
```
